256 devices in a mesh: island: 16 (over x, z_lo), expert: 4 (over y), fsdp: 4 (over z_hi, core).
Axes of the slice: x: 4, y: 4, z: 8 (z_hi: 2, z_lo: 4; z = z_hi * 4 + z_lo), core: 2. Of those that a mesh axis runs over, the one named last changes fastest.
Arguments:
- deltas: bfloat16 [16, 4, 4096, 1536], P('island', 'expert', 'fsdp'), may hold values from -6 to 6
- order: int32 [4], replicated, may hold values from 0 to 15
- staleness: int32 [16], replicated, may hold values from 0 to 15
- period: int32 [1], replicated, may hold values from 2 to 4
- counter: int32 [1], replicated, may hold values from 0 to 11
- theta: float32 [4, 4096, 1536], P('expert', ('fsdp', 'island')), may hold values from -6 to 6
- momentum: float32 [4, 4096, 1536], P('expert', ('fsdp', 'island')), may hold values from -4 to 4
- accum: float32 [4, 4096, 1536], P('expert', ('fsdp', 'island')), may hold values from -4 to 4
Outputs:
- fresh: bfloat16 [16, 4, 4096, 1536], P('island', 'expert', 'fsdp')
- theta_out: float32 [4, 4096, 1536], P('expert', ('fsdp', 'island'))
- momentum_out: float32 [4, 4096, 1536], P('expert', ('fsdp', 'island'))
- accum_out: float32 [4, 4096, 1536], P('expert', ('fsdp', 'island'))
The draws below stay inside these ranges and needn't reach their ends.
All inputs are finite; a program needn't handle non-finite values.
Results may differ from the reference program's by a relative error of at most 0.001.
Values may be sent and summed in bfloat16 or wider, within the bound.
A program may use at most 128 MiB of HBM per device.

```python
import jax
import jax.numpy as jnp
from jax import lax

D = 4096
FF = 1536
ARRIVALS = 4
EXPERTS = 4
N_ISLAND = 16


def touch_ends(drawn, stream_key, low, top_value):
    place = [jax.random.randint(jax.random.fold_in(stream_key, axis), (), 0, length) for axis, length in enumerate(drawn.shape)]
    widest = drawn.shape.index(max(drawn.shape))
    neighbour = place[:widest] + [(place[widest] + 1) % drawn.shape[widest]] + place[widest + 1:]
    return drawn.at[tuple(place)].set(low).at[tuple(neighbour)].set(top_value)


def block_scale(key, shape, cuts, least, high):
    loudness = 1.0
    for position, blocks in cuts:
        heights = jax.random.uniform(jax.random.fold_in(jax.random.fold_in(key, 6), position), (blocks,), jnp.float32, least / len(cuts), high / len(cuts))
        loudness = loudness * jnp.repeat(jnp.exp(heights), shape[position] // blocks).reshape((-1,) + (1,) * (len(shape) - 1 - position))
    return loudness


def centred(own_key, extent, deviation, limit, cuts=(), kind=jnp.bfloat16):
    entries = deviation * jax.random.normal(own_key, extent, jnp.float32)
    if cuts:
        entries = entries * block_scale(own_key, extent, cuts, -0.22, 0.18)
    return jnp.clip(entries, -limit, limit).astype(kind)


def setup_inputs(seed: int = 0) -> dict:
    arg_keys = jax.random.split(jax.random.key(seed), 9)
    return {
        "deltas": centred(arg_keys[0], (N_ISLAND, EXPERTS, D, FF), 1.0, 6.0, ((0, 16), (1, 4), (2, 4))),
        "order": touch_ends(jax.random.randint(arg_keys[1], (ARRIVALS,), 0, N_ISLAND), jax.random.fold_in(arg_keys[1], 1), 0, N_ISLAND - 1).astype(jnp.int32),
        "staleness": touch_ends(jax.random.randint(arg_keys[2], (N_ISLAND,), 0, 16), jax.random.fold_in(arg_keys[2], 1), 0, 15).astype(jnp.int32),
        "period": jax.random.randint(arg_keys[3], (1,), 2, 5).astype(jnp.int32),
        "counter": jax.random.randint(arg_keys[4], (1,), 0, 12).astype(jnp.int32),
        "theta": centred(arg_keys[5], (EXPERTS, D, FF), 1.0, 6.0, ((0, 4), (1, 64)), jnp.float32),
        "momentum": centred(arg_keys[6], (EXPERTS, D, FF), 0.5, 4.0, ((0, 4), (1, 64)), jnp.float32),
        "accum": centred(arg_keys[7], (EXPERTS, D, FF), 0.5, 4.0, ((0, 4), (1, 64)), jnp.float32),
    }


def reference(deltas, order, staleness, period, counter, theta, momentum, accum):
    rate = 0.7
    beta = 0.9
    fresh = jnp.zeros(deltas.shape, jnp.bfloat16)
    period_f = period[0].astype(jnp.float32)
    for k in range(ARRIVALS):
        source = order[k]
        weight = lax.rsqrt(1.0 + staleness[source].astype(jnp.float32) + k)
        grad = weight * deltas[source].astype(jnp.float32)
        boundary = (counter[0] + k + 1) % period[0] == 0
        correction = 1.0 - jnp.power(jnp.float32(beta), (counter[0] + k + 1).astype(jnp.float32))
        momentum = jnp.where(boundary, beta * momentum + accum / period_f, momentum)
        accum = jnp.where(boundary, grad, accum + grad)
        theta = theta - rate * (grad + jnp.where(boundary, beta * momentum / correction, jnp.float32(0.0)))
        fresh = fresh.at[source].set(theta.astype(jnp.bfloat16))
    return (fresh, theta, momentum, accum)
```

```python
import jax
import jax.numpy as jnp
from jax import lax
from jax.sharding import PartitionSpec as P


def local(deltas, order, staleness, period, counter, theta, momentum, accum):
    rate = 0.7
    beta = 0.9
    islands = lax.axis_size("island")
    rows_all, width = deltas.shape[2:]
    rows = rows_all // islands
    mine = deltas.reshape(islands, rows, width)
    pieces = lax.all_to_all(mine, "island", 0, 0, tiled=True)
    period_f = period[0].astype(jnp.float32)
    outgoing = jnp.zeros((islands, rows, width), jnp.bfloat16)
    for k in range(order.shape[0]):
        source = order[k]
        piece = lax.dynamic_index_in_dim(pieces, source, 0, keepdims=True)
        weight = lax.rsqrt(1.0 + staleness[source].astype(jnp.float32) + k)
        grad = weight * piece.astype(jnp.float32)
        boundary = (counter[0] + k + 1) % period[0] == 0
        correction = 1.0 - jnp.power(jnp.float32(beta), (counter[0] + k + 1).astype(jnp.float32))
        momentum = jnp.where(boundary, beta * momentum + accum / period_f, momentum)
        accum = jnp.where(boundary, grad, accum + grad)
        theta = theta - rate * (
            grad + jnp.where(boundary, beta * momentum / correction, jnp.float32(0.0))
        )
        outgoing = lax.dynamic_update_slice_in_dim(outgoing, theta.astype(jnp.bfloat16), source, 0)
    fresh = lax.all_to_all(outgoing, "island", 0, 0, tiled=True)
    return (fresh.reshape(deltas.shape), theta, momentum, accum)


def solution(mesh):
    state = P("expert", ("fsdp", "island"), None)
    replicas = P("island", "expert", "fsdp", None)
    return jax.shard_map(
        local,
        mesh=mesh,
        in_specs=(replicas, P(), P(), P(), P(), state, state, state),
        out_specs=(replicas, state, state, state),
        check_vma=False,
    )
```

```python
import functools

import jax
import jax.numpy as jnp
from jax import lax
from jax.experimental import pallas as pl
from jax.experimental.pallas import tpu as pltpu
from jax.sharding import PartitionSpec as P

RATE = 0.7
BETA = 0.9
LOG_BETA = -0.10536051565782628
ARRIVALS = 4
SIDE = 4
STEP = 16
HALVES = 1
LEAD = 1
MESH = pl.DeviceIdType.MESH


def column_tile(width):
    return 512 if width % 512 == 0 else 128


def kernel(slots, chunks, deltas, order, staleness, period, counter, theta, momentum, accum,
           fresh, theta_out, momentum_out, accum_out,
           landed, packed, pieces, rounded, answers, returned, outgoing, send, recv, near):
    me = lax.axis_index("island")
    x, z = me // SIDE, me % SIDE

    def along_x(d):
        return {"island": ((x + d) % SIDE) * SIDE + z}

    def along_z(d):
        return {"island": x * SIDE + (z + d) % SIDE}

    def remote(stage, j, d, src, dst, where):
        at = (stage * len(chunks) + j) * (SIDE - 1) + d - 1
        return pltpu.make_async_remote_copy(
            src_ref=src, dst_ref=dst, send_sem=send.at[at], recv_sem=recv.at[at],
            device_id=where, device_id_type=MESH)

    def block(j, column):
        row, col, wide = chunks[j]
        return (pl.ds(column * SIDE, SIDE), pl.ds(row, STEP), pl.ds(col, wide))

    def spread(j, d):
        return remote(0, j, d, deltas.at[block(j, (x + d) % SIDE)], landed[j].at[d], along_x(d))

    def spread_own(j):
        return pltpu.make_async_copy(deltas.at[block(j, x)], landed[j].at[0], near.at[j])

    def hand(j, d):
        return remote(1, j, d, packed[j].at[d], pieces[j].at[d], along_z(d))

    def answer(j, d):
        return remote(2, j, d, answers[j].at[d], returned[j].at[d], along_z(d))

    def deliver(j, d):
        return remote(3, j, d, outgoing[j].at[d], fresh.at[block(j, x)], along_x(d))

    def deliver_own(j):
        return pltpu.make_async_copy(outgoing[j].at[0], fresh.at[block(j, x)], near.at[len(chunks) + j])

    barrier = pltpu.get_barrier_semaphore()
    for d in range(1, SIDE):
        pl.semaphore_signal(barrier, inc=1, device_id=along_x(d), device_id_type=MESH)
        pl.semaphore_signal(barrier, inc=1, device_id=along_z(d), device_id_type=MESH)
    pl.semaphore_wait(barrier, 2 * (SIDE - 1))

    def start_spread(j):
        for d in range(1, SIDE):
            spread(j, d).start()
        spread_own(j).start()

    for j in range(min(LEAD, len(chunks))):
        start_spread(j)

    zero = jnp.int32(0)
    who = [order[k] for k in range(ARRIVALS)]
    col = [w // SIDE for w in who]
    plane = [w % SIDE for w in who]
    slot, first = [], []
    for k in range(ARRIVALS):
        again, rank = zero, zero
        same = zero
        for l in range(k):
            hit = (who[l] == who[k]).astype(jnp.int32)
            again = jnp.maximum(again, hit)
            same = jnp.where(hit == 1, slot[l], same)
            rank = rank + first[l] * (plane[l] == plane[k]).astype(jnp.int32)
        first.append(1 - again)
        slot.append(jnp.where(again == 1, same, rank))

    def held(at_plane, s):
        return [((plane[k] == at_plane) & (slot[k] == s)) for k in range(ARRIVALS)]

    mine = []
    for s in range(slots):
        value = zero
        for k, hit in enumerate(held(z, s)):
            value = jnp.where(hit, (x - col[k] + SIDE) % SIDE, value)
        mine.append(value)
    last = []
    for d in range(SIDE):
        row = []
        for s in range(slots):
            value = zero
            for k, hit in enumerate(held((z + d) % SIDE, s)):
                value = jnp.where(hit, jnp.int32(k), value)
            row.append(value)
        last.append(row)
    place = []
    for d in range(SIDE):
        value = jnp.int32(-1)
        for k in range(ARRIVALS):
            value = jnp.where((plane[k] == z) & (col[k] == (x + d) % SIDE), slot[k], value)
        place.append(value)
    origin = [(z - plane[k] + SIDE) % SIDE for k in range(ARRIVALS)]

    def pack(j):
        for d in range(1, SIDE):
            spread(j, d).wait_recv()
        spread_own(j).wait()
        for d in (2, 1, 3, 0):
            target = pieces[j] if d == 0 else packed[j]
            for s in range(slots):
                target[d, s] = landed[j][mine[s], (z + d) % SIDE]
            if d:
                hand(j, d).start()

    count = counter[0]
    every = period[0]

    def update(j):
        for d in range(1, SIDE):
            hand(j, d).wait_recv()
        row, begin, wide = chunks[j]
        tile = column_tile(wide)
        for start in range(0, wide, tile):
            here = (pl.ds(row, STEP), pl.ds(begin + start, tile))
            part = pl.ds(start, tile)
            th, mo, ac = theta[here], momentum[here], accum[here]
            one = jnp.ones((1, tile), jnp.float32)
            inverse = 1.0 / (one * every.astype(jnp.float32))
            for k in range(ARRIVALS):
                weight = lax.rsqrt(one * (1.0 + staleness[who[k]].astype(jnp.float32) + k))
                step = count + (k + 1)
                boundary = lax.rem(step, every) == 0
                factor = BETA / (1.0 - jnp.exp(one * (step.astype(jnp.float32) * LOG_BETA)))
                piece = pieces[j][origin[k], slot[k], :, part]
                grad = weight * piece.astype(jnp.float32)
                mo = jnp.where(boundary, BETA * mo + ac * inverse, mo)
                ac = jnp.where(boundary, grad, ac + grad)
                th = th - RATE * (grad + jnp.where(boundary, factor * mo, 0.0))
                rounded[j][k, :, part] = th.astype(jnp.bfloat16)
            theta_out[here], momentum_out[here], accum_out[here] = th, mo, ac
        for d in (2, 1, 3, 0):
            target = returned[j] if d == 0 else answers[j]
            for s in range(slots):
                target[d, s] = rounded[j][last[d][s]]
            if d:
                answer(j, d).start()

    def forward(j):
        for d in range(1, SIDE):
            answer(j, d).wait_recv()
        for d in (2, 1, 3, 0):
            keep = place[d] >= 0
            at = jnp.maximum(place[d], 0)
            for owner in range(SIDE):
                block = returned[j][(z - owner + SIDE) % SIDE, at]
                outgoing[j][d, owner] = jnp.where(keep, block, jnp.zeros_like(block))
            if d:
                deliver(j, d).start()
            else:
                deliver_own(j).start()

    total = len(chunks)
    for t in range(total + 2):
        if t + LEAD < total:
            start_spread(t + LEAD)
        if t < total:
            pack(t)
        if 0 <= t - 1 < total:
            update(t - 1)
        if 0 <= t - 2 < total:
            forward(t - 2)
    for j in range(total):
        for d in range(1, SIDE):
            deliver(j, d).wait_recv()
            for stage in (spread, hand, answer, deliver):
                stage(j, d).wait_send()
        deliver_own(j).wait()


def run(slots, tag, deltas, order, staleness, period, counter, theta, momentum, accum):
    islands, rows, width = deltas.shape
    wide = width // HALVES
    chunks = [(r, c * wide, wide) for r in range(0, rows, STEP) for c in range(HALVES)]
    n = len(chunks)
    copies = 4 * n * (SIDE - 1)
    smem = pl.BlockSpec(memory_space=pltpu.SMEM)
    vmem = pl.BlockSpec(memory_space=pltpu.VMEM)
    hbm = pl.BlockSpec(memory_space=pl.ANY)
    half = lambda *lead: [pltpu.VMEM((*lead, STEP, wide), jnp.bfloat16) for _ in range(n)]
    state = jax.ShapeDtypeStruct(theta.shape, jnp.float32)
    return pl.pallas_call(
        functools.partial(kernel, slots, chunks),
        out_shape=(jax.ShapeDtypeStruct(deltas.shape, jnp.bfloat16), state, state, state),
        in_specs=[hbm, smem, smem, smem, smem, vmem, vmem, vmem],
        out_specs=(hbm, vmem, vmem, vmem),
        scratch_shapes=[
            half(SIDE, SIDE),
            half(SIDE, slots),
            half(SIDE, slots),
            half(ARRIVALS),
            half(SIDE, slots),
            half(SIDE, slots),
            half(SIDE, SIDE),
            pltpu.SemaphoreType.DMA((copies,)),
            pltpu.SemaphoreType.DMA((copies,)),
            pltpu.SemaphoreType.DMA((2 * n,)),
        ],
        compiler_params=pltpu.CompilerParams(
            collective_id=tag, has_side_effects=True, vmem_limit_bytes=48 * 1024 * 1024
        ),
    )(deltas, order, staleness, period, counter, theta, momentum, accum)


def local(deltas, order, staleness, period, counter, theta, momentum, accum):
    islands = lax.axis_size("island")
    rows_all, width = deltas.shape[2:]
    blocks = deltas.reshape(islands, rows_all // islands, width)
    replica = jnp.arange(islands)
    arrives = (order[:, None] == replica[None, :]).any(0)
    crowd = arrives.reshape(SIDE, SIDE).sum(0).max()
    args = (blocks, order, staleness, period, counter, theta[0], momentum[0], accum[0])
    fresh, theta, momentum, accum = lax.cond(
        crowd <= 2, functools.partial(run, 2, 0), functools.partial(run, ARRIVALS, 1), *args
    )
    return (fresh.reshape(deltas.shape), theta[None], momentum[None], accum[None])


def solution(mesh):
    state = P("expert", ("fsdp", "island"), None)
    replicas = P("island", "expert", "fsdp", None)
    return jax.shard_map(
        local,
        mesh=mesh,
        in_specs=(replicas, P(), P(), P(), P(), state, state, state),
        out_specs=(replicas, state, state, state),
        check_vma=False,
    )
```

```python
import functools

import jax
import jax.numpy as jnp
from jax import lax
from jax.experimental import pallas as pl
from jax.experimental.pallas import tpu as pltpu
from jax.sharding import PartitionSpec as P

RATE = 0.7
BETA = 0.9
LOG_BETA = -0.10536051565782628
ARRIVALS = 4
SIDE = 4
STEP = 16
HALVES = 2
LEAD = 3
PLANS = ((2, 1, 1, 2), (1, 2, 2, 1), (2, 2, 2, 2), (4, 4, 4, 4))
MESH = pl.DeviceIdType.MESH


def column_tile(width):
    return 512 if width % 512 == 0 else 128


def kernel(room, chunks, deltas, order, staleness, period, counter, theta, momentum, accum,
           fresh, theta_out, momentum_out, accum_out,
           landed, packed, pieces, rounded, answers, returned, outgoing, send, recv, near):
    me = lax.axis_index("island")
    x, z = me // SIDE, me % SIDE
    slots, least = max(room), min(room)
    groups = [(0, least)] + [(s, 1) for s in range(least, slots)]

    def where_room(s, plane, go):
        if s < least:
            go()
        else:
            has = functools.reduce(jnp.logical_or, [plane == p for p in range(SIDE) if room[p] > s])
            pl.when(has)(go)

    def along_x(d):
        return {"island": ((x + d) % SIDE) * SIDE + z}

    def along_z(d):
        return {"island": x * SIDE + (z + d) % SIDE}

    def remote(stage, j, d, src, dst, where):
        at = stage * (SIDE - 1) + d - 1
        return pltpu.make_async_remote_copy(
            src_ref=src, dst_ref=dst, send_sem=send.at[j, at], recv_sem=recv.at[j, at],
            device_id=where, device_id_type=MESH)

    def block(j, column):
        row, col, wide = chunks[j]
        return (pl.ds(column * SIDE, SIDE), pl.ds(row, STEP), pl.ds(col, wide))

    def spread(j, d):
        return remote(0, j, d, deltas.at[block(j, (x + d) % SIDE)], landed[j].at[d], along_x(d))

    def spread_own(j):
        return pltpu.make_async_copy(deltas.at[block(j, x)], landed[j].at[0], near.at[j])

    def hand(j, d, g):
        part = pl.ds(*groups[g])
        return remote(2 + g, j, d, packed[j].at[d, part], pieces[j].at[d, part], along_z(d))

    def answer(j, d, g):
        part = pl.ds(*groups[g])
        return remote(2 + len(groups) + g, j, d, answers[j].at[d, part], returned[j].at[d, part], along_z(d))

    def over_groups(plane, act):
        for g, (s, _) in enumerate(groups):
            where_room(s, plane, functools.partial(act, g))

    def deliver(j, d):
        return remote(1, j, d, outgoing[j].at[d], fresh.at[block(j, x)], along_x(d))

    def deliver_own(j):
        return pltpu.make_async_copy(outgoing[j].at[0], fresh.at[block(j, x)], near.at[len(chunks) + j])

    barrier = pltpu.get_barrier_semaphore()
    for d in range(1, SIDE):
        pl.semaphore_signal(barrier, inc=1, device_id=along_x(d), device_id_type=MESH)
        pl.semaphore_signal(barrier, inc=1, device_id=along_z(d), device_id_type=MESH)
    pl.semaphore_wait(barrier, 2 * (SIDE - 1))

    def start_spread(j):
        for d in range(1, SIDE):
            spread(j, d).start()
        spread_own(j).start()

    for j in range(min(LEAD, len(chunks))):
        start_spread(j)

    zero = jnp.int32(0)
    who = [order[k] for k in range(ARRIVALS)]
    col = [w // SIDE for w in who]
    plane = [w % SIDE for w in who]
    slot, first = [], []
    for k in range(ARRIVALS):
        again, rank = zero, zero
        same = zero
        for l in range(k):
            hit = (who[l] == who[k]).astype(jnp.int32)
            again = jnp.maximum(again, hit)
            same = jnp.where(hit == 1, slot[l], same)
            rank = rank + first[l] * (plane[l] == plane[k]).astype(jnp.int32)
        first.append(1 - again)
        slot.append(jnp.where(again == 1, same, rank))

    def held(at_plane, s):
        return [((plane[k] == at_plane) & (slot[k] == s)) for k in range(ARRIVALS)]

    mine = []
    for s in range(slots):
        value = zero
        for k, hit in enumerate(held(z, s)):
            value = jnp.where(hit, (x - col[k] + SIDE) % SIDE, value)
        mine.append(value)
    last = []
    for d in range(SIDE):
        row = []
        for s in range(slots):
            value = zero
            for k, hit in enumerate(held((z + d) % SIDE, s)):
                value = jnp.where(hit, jnp.int32(k), value)
            row.append(value)
        last.append(row)
    place = []
    for d in range(SIDE):
        value = jnp.int32(-1)
        for k in range(ARRIVALS):
            value = jnp.where((plane[k] == z) & (col[k] == (x + d) % SIDE), slot[k], value)
        place.append(value)
    origin = [(z - plane[k] + SIDE) % SIDE for k in range(ARRIVALS)]

    def pack(j):
        for d in range(1, SIDE):
            spread(j, d).wait_recv()
        spread_own(j).wait()
        for d in (2, 1, 3, 0):
            target = pieces[j] if d == 0 else packed[j]
            for s in range(slots):
                target[d, s] = landed[j][mine[s], (z + d) % SIDE]
            if d:
                over_groups(z, lambda g, d=d: hand(j, d, g).start())

    count = counter[0]
    every = period[0]

    def update(j):
        for d in range(1, SIDE):
            over_groups((z + SIDE - d) % SIDE, lambda g, d=d: hand(j, d, g).wait_recv())
        row, begin, wide = chunks[j]
        tile = column_tile(wide)
        for start in range(0, wide, tile):
            here = (pl.ds(row, STEP), pl.ds(begin + start, tile))
            part = pl.ds(start, tile)
            th, mo, ac = theta[here], momentum[here], accum[here]
            one = jnp.ones((1, tile), jnp.float32)
            inverse = 1.0 / (one * every.astype(jnp.float32))
            for k in range(ARRIVALS):
                weight = lax.rsqrt(one * (1.0 + staleness[who[k]].astype(jnp.float32) + k))
                step = count + (k + 1)
                boundary = lax.rem(step, every) == 0
                factor = BETA / (1.0 - jnp.exp(one * (step.astype(jnp.float32) * LOG_BETA)))
                piece = pieces[j][origin[k], slot[k], :, part]
                grad = weight * piece.astype(jnp.float32)
                mo = jnp.where(boundary, BETA * mo + ac * inverse, mo)
                ac = jnp.where(boundary, grad, ac + grad)
                th = th - RATE * (grad + jnp.where(boundary, factor * mo, 0.0))
                rounded[j][k, :, part] = th.astype(jnp.bfloat16)
            theta_out[here], momentum_out[here], accum_out[here] = th, mo, ac
        for d in (2, 1, 3, 0):
            target = returned[j] if d == 0 else answers[j]
            for s in range(slots):
                target[d, s] = rounded[j][last[d][s]]
            if d:
                over_groups((z + d) % SIDE, lambda g, d=d: answer(j, d, g).start())

    def forward(j):
        for d in range(1, SIDE):
            over_groups(z, lambda g, d=d: answer(j, d, g).wait_recv())
        for d in (2, 1, 3, 0):
            keep = place[d] >= 0
            at = jnp.maximum(place[d], 0)
            for owner in range(SIDE):
                block = returned[j][(z - owner + SIDE) % SIDE, at]
                outgoing[j][d, owner] = jnp.where(keep, block, jnp.zeros_like(block))
            if d:
                deliver(j, d).start()
            else:
                deliver_own(j).start()

    total = len(chunks)
    for t in range(total + 2):
        if t + LEAD < total:
            start_spread(t + LEAD)
        if t < total:
            pack(t)
        if 0 <= t - 1 < total:
            update(t - 1)
        if 0 <= t - 2 < total:
            forward(t - 2)
    for j in range(total):
        for d in range(1, SIDE):
            deliver(j, d).wait_recv()
            spread(j, d).wait_send()
            deliver(j, d).wait_send()
            over_groups(z, lambda g, d=d: hand(j, d, g).wait_send())
            over_groups((z + d) % SIDE, lambda g, d=d: answer(j, d, g).wait_send())
        deliver_own(j).wait()


def run(room, tag, deltas, order, staleness, period, counter, theta, momentum, accum):
    islands, rows, width = deltas.shape
    wide = width // HALVES
    chunks = [(r, c * wide, wide) for r in range(0, rows, STEP) for c in range(HALVES)]
    n = len(chunks)
    slots = max(room)
    stages = 2 + 2 * (1 + slots - min(room))
    copies = (n, stages * (SIDE - 1))
    smem = pl.BlockSpec(memory_space=pltpu.SMEM)
    vmem = pl.BlockSpec(memory_space=pltpu.VMEM)
    hbm = pl.BlockSpec(memory_space=pl.ANY)
    half = lambda *lead: [pltpu.VMEM((*lead, STEP, wide), jnp.bfloat16) for _ in range(n)]
    state = jax.ShapeDtypeStruct(theta.shape, jnp.float32)
    return pl.pallas_call(
        functools.partial(kernel, room, chunks),
        out_shape=(jax.ShapeDtypeStruct(deltas.shape, jnp.bfloat16), state, state, state),
        in_specs=[hbm, smem, smem, smem, smem, vmem, vmem, vmem],
        out_specs=(hbm, vmem, vmem, vmem),
        scratch_shapes=[
            half(SIDE, SIDE),
            half(SIDE, slots),
            half(SIDE, slots),
            half(ARRIVALS),
            half(SIDE, slots),
            half(SIDE, slots),
            half(SIDE, SIDE),
            pltpu.SemaphoreType.DMA(copies),
            pltpu.SemaphoreType.DMA(copies),
            pltpu.SemaphoreType.DMA((2 * n,)),
        ],
        compiler_params=pltpu.CompilerParams(
            collective_id=tag, has_side_effects=True, vmem_limit_bytes=48 * 1024 * 1024
        ),
    )(deltas, order, staleness, period, counter, theta, momentum, accum)


def local(deltas, order, staleness, period, counter, theta, momentum, accum):
    islands = lax.axis_size("island")
    rows_all, width = deltas.shape[2:]
    blocks = deltas.reshape(islands, rows_all // islands, width)
    arrives = (order[:, None] == jnp.arange(islands)[None, :]).any(0)
    crowd = arrives.reshape(SIDE, SIDE).sum(0)
    args = (blocks, order, staleness, period, counter, theta[0], momentum[0], accum[0])
    branches = [functools.partial(run, room, tag) for tag, room in enumerate(PLANS)]
    fits = (crowd[None, :] <= jnp.array(PLANS)).all(1)
    fresh, theta, momentum, accum = lax.switch(jnp.argmax(fits).astype(jnp.int32), branches, *args)
    return (fresh.reshape(deltas.shape), theta[None], momentum[None], accum[None])


def solution(mesh):
    state = P("expert", ("fsdp", "island"), None)
    replicas = P("island", "expert", "fsdp", None)
    return jax.shard_map(
        local,
        mesh=mesh,
        in_specs=(replicas, P(), P(), P(), P(), state, state, state),
        out_specs=(replicas, state, state, state),
        check_vma=False,
    )
```

```python
import functools

import jax
import jax.numpy as jnp
from jax import lax
from jax.experimental import pallas as pl
from jax.experimental.pallas import tpu as pltpu
from jax.sharding import PartitionSpec as P

RATE = 0.7
BETA = 0.9
LOG_BETA = -0.10536051565782628
ARRIVALS = 4
SIDE = 4
STEP = 16
HALVES = 2
LEAD = 3
PLANS = ((2, 1, 1, 2), (1, 2, 2, 1), (2, 2, 2, 2), (4, 4, 4, 4))
SETTLE = 2
MESH = pl.DeviceIdType.MESH


def column_tile(width):
    return 512 if width % 512 == 0 else 128


def kernel(room, chunks, deltas, order, staleness, period, counter, theta, momentum, accum,
           fresh, theta_out, momentum_out, accum_out,
           state, landed, packed, pieces, rounded, answers, returned, outgoing, send, recv, near, moved):
    me = lax.axis_index("island")
    x, z = me // SIDE, me % SIDE
    slots, least = max(room), min(room)
    groups = [(0, least)] + [(s, 1) for s in range(least, slots)]

    def where_room(s, plane, go):
        if s < least:
            go()
        else:
            has = functools.reduce(jnp.logical_or, [plane == p for p in range(SIDE) if room[p] > s])
            pl.when(has)(go)

    def along_x(d):
        return {"island": ((x + d) % SIDE) * SIDE + z}

    def along_z(d):
        return {"island": x * SIDE + (z + d) % SIDE}

    def remote(stage, j, d, src, dst, where):
        at = stage * (SIDE - 1) + d - 1
        return pltpu.make_async_remote_copy(
            src_ref=src, dst_ref=dst, send_sem=send.at[j, at], recv_sem=recv.at[j, at],
            device_id=where, device_id_type=MESH)

    def block(j, column):
        row, col, wide = chunks[j]
        return (pl.ds(column * SIDE, SIDE), pl.ds(row, STEP), pl.ds(col, wide))

    def spread(j, d):
        return remote(0, j, d, deltas.at[block(j, (x + d) % SIDE)], landed[j].at[d], along_x(d))

    def spread_own(j):
        return pltpu.make_async_copy(deltas.at[block(j, x)], landed[j].at[0], near.at[j])

    def hand(j, d, g):
        part = pl.ds(*groups[g])
        return remote(2 + g, j, d, packed[j].at[d, part], pieces[j].at[d, part], along_z(d))

    def answer(j, d, g):
        part = pl.ds(*groups[g])
        return remote(2 + len(groups) + g, j, d, answers[j].at[d, part], returned[j].at[d, part], along_z(d))

    def over_groups(plane, act):
        for g, (s, _) in enumerate(groups):
            where_room(s, plane, functools.partial(act, g))

    def deliver(j, d):
        return remote(1, j, d, outgoing[j].at[d], fresh.at[block(j, x)], along_x(d))

    def deliver_own(j):
        return pltpu.make_async_copy(outgoing[j].at[0], fresh.at[block(j, x)], near.at[len(chunks) + j])

    theta_now, momentum_now, accum_now = state
    loads = [pltpu.make_async_copy(src, dst, moved.at[len(chunks), i])
             for i, (src, dst) in enumerate(zip((theta, momentum, accum), state))]
    for load in loads:
        load.start()

    def store(j):
        row, col, wide = chunks[j]
        here = (pl.ds(row, STEP), pl.ds(col, wide))
        return [pltpu.make_async_copy(src.at[here], dst.at[here], moved.at[j, i])
                for i, (src, dst) in enumerate(zip(state, (theta_out, momentum_out, accum_out)))]

    barrier = pltpu.get_barrier_semaphore()
    for d in range(1, SIDE):
        pl.semaphore_signal(barrier, inc=1, device_id=along_x(d), device_id_type=MESH)
        pl.semaphore_signal(barrier, inc=1, device_id=along_z(d), device_id_type=MESH)
    pl.semaphore_wait(barrier, 2 * (SIDE - 1))

    def start_spread(j):
        for d in range(1, SIDE):
            spread(j, d).start()
        spread_own(j).start()

    for j in range(min(LEAD, len(chunks))):
        start_spread(j)

    zero = jnp.int32(0)
    who = [order[k] for k in range(ARRIVALS)]
    col = [w // SIDE for w in who]
    plane = [w % SIDE for w in who]
    slot, first = [], []
    for k in range(ARRIVALS):
        again, rank = zero, zero
        same = zero
        for l in range(k):
            hit = (who[l] == who[k]).astype(jnp.int32)
            again = jnp.maximum(again, hit)
            same = jnp.where(hit == 1, slot[l], same)
            rank = rank + first[l] * (plane[l] == plane[k]).astype(jnp.int32)
        first.append(1 - again)
        slot.append(jnp.where(again == 1, same, rank))

    def held(at_plane, s):
        return [((plane[k] == at_plane) & (slot[k] == s)) for k in range(ARRIVALS)]

    mine = []
    for s in range(slots):
        value = zero
        for k, hit in enumerate(held(z, s)):
            value = jnp.where(hit, (x - col[k] + SIDE) % SIDE, value)
        mine.append(value)
    last = []
    for d in range(SIDE):
        row = []
        for s in range(slots):
            value = zero
            for k, hit in enumerate(held((z + d) % SIDE, s)):
                value = jnp.where(hit, jnp.int32(k), value)
            row.append(value)
        last.append(row)
    place = []
    for d in range(SIDE):
        value = jnp.int32(-1)
        for k in range(ARRIVALS):
            value = jnp.where((plane[k] == z) & (col[k] == (x + d) % SIDE), slot[k], value)
        place.append(value)
    origin = [(z - plane[k] + SIDE) % SIDE for k in range(ARRIVALS)]

    def pack(j):
        for d in range(1, SIDE):
            spread(j, d).wait_recv()
        spread_own(j).wait()
        for d in (2, 1, 3, 0):
            target = pieces[j] if d == 0 else packed[j]
            for s in range(slots):
                target[d, s] = landed[j][mine[s], (z + d) % SIDE]
            if d:
                over_groups(z, lambda g, d=d: hand(j, d, g).start())

    count = counter[0]
    every = period[0]

    def update(j):
        for d in range(1, SIDE):
            over_groups((z + SIDE - d) % SIDE, lambda g, d=d: hand(j, d, g).wait_recv())
        if j == 0:
            for load in loads:
                load.wait()
        row, begin, wide = chunks[j]
        tile = column_tile(wide)
        for start in range(0, wide, tile):
            here = (pl.ds(row, STEP), pl.ds(begin + start, tile))
            part = pl.ds(start, tile)
            th, mo, ac = theta_now[here], momentum_now[here], accum_now[here]
            one = jnp.ones((1, tile), jnp.float32)
            inverse = 1.0 / (one * every.astype(jnp.float32))
            for k in range(ARRIVALS):
                weight = lax.rsqrt(one * (1.0 + staleness[who[k]].astype(jnp.float32) + k))
                step = count + (k + 1)
                boundary = lax.rem(step, every) == 0
                factor = BETA / (1.0 - jnp.exp(one * (step.astype(jnp.float32) * LOG_BETA)))
                piece = pieces[j][origin[k], slot[k], :, part]
                grad = weight * piece.astype(jnp.float32)
                mo = jnp.where(boundary, BETA * mo + ac * inverse, mo)
                ac = jnp.where(boundary, grad, ac + grad)
                th = th - RATE * (grad + jnp.where(boundary, factor * mo, 0.0))
                rounded[j][k, :, part] = th.astype(jnp.bfloat16)
            theta_now[here], momentum_now[here], accum_now[here] = th, mo, ac
        for d in (2, 1, 3, 0):
            target = returned[j] if d == 0 else answers[j]
            for s in range(slots):
                target[d, s] = rounded[j][last[d][s]]
            if d:
                over_groups((z + d) % SIDE, lambda g, d=d: answer(j, d, g).start())

    def forward(j):
        for d in range(1, SIDE):
            over_groups(z, lambda g, d=d: answer(j, d, g).wait_recv())
        for copy in store(j):
            copy.start()
        for d in (2, 1, 3, 0):
            keep = place[d] >= 0
            at = jnp.maximum(place[d], 0)
            for owner in range(SIDE):
                block = returned[j][(z - owner + SIDE) % SIDE, at]
                outgoing[j][d, owner] = jnp.where(keep, block, jnp.zeros_like(block))
            if d:
                deliver(j, d).start()
            else:
                deliver_own(j).start()

    total = len(chunks)
    for t in range(total + 2):
        if t + LEAD < total:
            start_spread(t + LEAD)
        if t < total:
            pack(t)
        if 0 <= t - 1 < total:
            update(t - 1)
        if 0 <= t - 2 < total:
            forward(t - 2)
    for j in range(total):
        for d in range(1, SIDE):
            deliver(j, d).wait_recv()
            spread(j, d).wait_send()
            deliver(j, d).wait_send()
            over_groups(z, lambda g, d=d: hand(j, d, g).wait_send())
            over_groups((z + d) % SIDE, lambda g, d=d: answer(j, d, g).wait_send())
        deliver_own(j).wait()
        for copy in store(j):
            copy.wait()


def run(room, tag, deltas, order, staleness, period, counter, theta, momentum, accum):
    islands, rows, width = deltas.shape
    wide = width // HALVES
    chunks = [(r, c * wide, wide) for r in range(0, rows, STEP) for c in range(HALVES)]
    n = len(chunks)
    slots = max(room)
    stages = 2 + 2 * (1 + slots - min(room))
    copies = (n, stages * (SIDE - 1))
    smem = pl.BlockSpec(memory_space=pltpu.SMEM)
    hbm = pl.BlockSpec(memory_space=pl.ANY)
    half = lambda *lead: [pltpu.VMEM((*lead, STEP, wide), jnp.bfloat16) for _ in range(n)]
    state = jax.ShapeDtypeStruct(theta.shape, jnp.float32)
    return pl.pallas_call(
        functools.partial(kernel, room, chunks),
        out_shape=(jax.ShapeDtypeStruct(deltas.shape, jnp.bfloat16), state, state, state),
        in_specs=[hbm, smem, smem, smem, smem, hbm, hbm, hbm],
        out_specs=(hbm, hbm, hbm, hbm),
        scratch_shapes=[
            [pltpu.VMEM(theta.shape, jnp.float32) for _ in range(3)],
            half(SIDE, SIDE),
            half(SIDE, slots),
            half(SIDE, slots),
            half(ARRIVALS),
            half(SIDE, slots),
            half(SIDE, slots),
            half(SIDE, SIDE),
            pltpu.SemaphoreType.DMA(copies),
            pltpu.SemaphoreType.DMA(copies),
            pltpu.SemaphoreType.DMA((2 * n,)),
            pltpu.SemaphoreType.DMA((n + 1, 3)),
        ],
        compiler_params=pltpu.CompilerParams(
            collective_id=tag, has_side_effects=True, vmem_limit_bytes=48 * 1024 * 1024
        ),
    )(deltas, order, staleness, period, counter, theta, momentum, accum)


def settle_kernel(*refs):
    half = len(refs) // 2
    for src, dst in zip(refs[:half], refs[half:]):
        dst[...] = src[...]


def settle(*results):
    def spec(r):
        shape = (r.shape[0] // SETTLE, *r.shape[1:])
        return pl.BlockSpec(shape, lambda i: (i,) + (0,) * (r.ndim - 1))

    specs = tuple(spec(r) for r in results)
    return pl.pallas_call(
        settle_kernel,
        grid=(SETTLE,),
        out_shape=tuple(jax.ShapeDtypeStruct(r.shape, r.dtype) for r in results),
        in_specs=specs,
        out_specs=specs,
        compiler_params=pltpu.CompilerParams(vmem_limit_bytes=48 * 1024 * 1024),
    )(*results)


def local(deltas, order, staleness, period, counter, theta, momentum, accum):
    islands = lax.axis_size("island")
    rows_all, width = deltas.shape[2:]
    blocks = deltas.reshape(islands, rows_all // islands, width)
    arrives = (order[:, None] == jnp.arange(islands)[None, :]).any(0)
    crowd = arrives.reshape(SIDE, SIDE).sum(0)
    args = (blocks, order, staleness, period, counter, theta[0], momentum[0], accum[0])
    branches = [functools.partial(run, room, tag) for tag, room in enumerate(PLANS)]
    fits = (crowd[None, :] <= jnp.array(PLANS)).all(1)
    results = lax.switch(jnp.argmax(fits).astype(jnp.int32), branches, *args)
    fresh, theta, momentum, accum = settle(*results)
    return (fresh.reshape(deltas.shape), theta[None], momentum[None], accum[None])


def solution(mesh):
    state = P("expert", ("fsdp", "island"), None)
    replicas = P("island", "expert", "fsdp", None)
    return jax.shard_map(
        local,
        mesh=mesh,
        in_specs=(replicas, P(), P(), P(), P(), state, state, state),
        out_specs=(replicas, state, state, state),
        check_vma=False,
    )
```
